32 devices in a mesh: dp: 8 (over z, core), ctx: 4 (over y, x).
Axes of the slice: x: 2, y: 2, z: 4, core: 2. Of those that a mesh axis runs over, the one named last changes fastest.
Arguments:
- hidden: bfloat16 [8, 512, 4096], P('dp', 'ctx'), may hold values from -6 to 6
- queries: bfloat16 [8, 512, 4096], P('dp', 'ctx'), may hold values from -6 to 6
- keys: bfloat16 [8, 512, 256], P('dp', 'ctx'), may hold values from -6 to 6
- values: bfloat16 [8, 512, 256], P('dp', 'ctx'), may hold values from -24 to 24
- out_weight: bfloat16 [4096, 4096], P(None, 'ctx'), may hold values from -0.09375 to 0.09375
- norm_gain: float32 [4096], replicated, may hold values from 0.1 to 1.9
- routes: int32 [8, 512, 8], P('dp', 'ctx'), may hold values from 0 to 31, all different within a row; in each aligned block of 128 rows (0 to 127, 128 to 255, ..., all dimensions but the last counted through in order) at most 36 rows name the same one
- slot_scores: float32 [8, 512, 8], P('dp', 'ctx'), may hold values from 0.1 to 1
- gate_weight: bfloat16 [32, 4096, 768], P(('dp', 'ctx')), may hold values from -0.09375 to 0.09375
- up_weight: bfloat16 [32, 4096, 768], P(('dp', 'ctx')), may hold values from -0.09375 to 0.09375
- down_weight: bfloat16 [32, 768, 4096], P(('dp', 'ctx')), may hold values from -0.21875 to 0.21875
Outputs:
- output: bfloat16 [8, 512, 4096], P('dp', 'ctx')
The draws below stay inside these ranges and needn't reach their ends.
Inputs may be any that keep to these rules, and one draw needn't show every extreme that they name: In each aligned block of 128 tokens (the tokens of one device, sequences in order) no expert is named by more than 36 of the block's routes, a bound that some block reaches.
All inputs are finite; a program needn't handle non-finite values.
Results may differ from the reference program's by a relative error of at most 0.0065.
Values may be sent and summed in bfloat16 or wider, within the bound.
A program may use at most 192 MiB of HBM per device.

```python
import math
import jax
import jax.numpy as jnp
import numpy as np
from jax import lax

D = 4096
HQ = 32
KVH = 2
DH = 128
HID = 768
TOP = 8
TOK_DEV = 128
SEQ = 512
SEQS = 8
EXPERTS = 32
CAP = 36
N_DP = 8
N_CTX = 4


def draw_queries(key, part):
    sample_key = jax.random.fold_in(key, 3)
    sample = jnp.clip(jax.random.normal(sample_key, (SEQS, SEQ, HQ * DH), jnp.float32), -6.0, 6.0)
    return sample.astype(jnp.bfloat16)


def draw_keys(key, part):
    sample_key = jax.random.fold_in(key, 5)
    sample = jnp.clip(jax.random.normal(sample_key, (SEQS, SEQ, KVH * DH), jnp.float32), -6.0, 6.0)
    return sample.astype(jnp.bfloat16)


def block_scale(rng, dims, split, smallest, high):
    def one(dim, parts):
        steps = jax.random.uniform(jax.random.fold_in(jax.random.fold_in(rng, 6), dim), (parts,), jnp.float32, smallest / len(split), high / len(split))
        return jnp.repeat(jnp.exp(steps), dims[dim] // parts).reshape((-1,) + (1,) * (len(dims) - dim - 1))

    gain = one(*split[0])
    for cut in split[1:]:
        gain = gain * one(*cut)
    return gain


def routed_block(stream_key, own, number, rows, count, top, bound, lean):
    ranking = jax.random.permutation(stream_key, count)
    heavy_load, common = portions_of(count, rows * top, bound, lean, True), portions_of(count, rows * top, bound, lean, False)
    places = jnp.arange(count)

    def named(lengths, rotation):
        used = int((lengths > 0).sum())
        fixed = max(1, used // 4)
        moved = fixed + (places - fixed + rotation * (used - fixed)) % max(1, count - fixed)
        return jnp.zeros((count,), jnp.int32).at[ranking[jnp.where(places < fixed, places, moved)]].set(jnp.asarray(lengths, jnp.int32))

    lengths = jnp.where(number % 4 == 0, named(heavy_load, number // 4), named(common, number - number // 4 - 1))
    mixed = jax.random.permutation(jax.random.fold_in(own, 3), count)
    donor, taker = mixed[0:count // 2 * 2:2], mixed[1:count // 2 * 2:2]
    room = jnp.minimum(lengths[donor] - 1, bound - lengths[taker]) // 2
    room = jnp.where((donor == ranking[0]) | (taker == ranking[0]) | (lengths[taker] == 0), 0, jnp.maximum(room, 0))
    moved = jax.random.randint(jax.random.fold_in(own, 4), (count // 2,), 0, 1 << 20) % (room + 1)
    lengths = lengths.at[donor].add(-moved).at[taker].add(moved)
    labels = jnp.searchsorted(jnp.cumsum(lengths), jnp.arange(rows * top), side="right").astype(jnp.int32)
    grid = labels.reshape(top, rows).T
    grid = grid[jax.random.permutation(jax.random.fold_in(own, 1), rows)]
    rotation = jax.random.randint(jax.random.fold_in(own, 2), (rows, 1), 0, top)
    return jnp.take_along_axis(grid, (jnp.arange(top)[None, :] + rotation) % top, axis=1)


def portions_of(count, total, reach, skew, full):
    loads = [(1 << 20) // math.isqrt(grade ** skew) + 1 for grade in range(1, count + 1)]
    largest = reach if full else min(reach, max(-(-total // count), total * loads[0] // sum(loads)))
    least = 1 if total - largest >= count - 1 else 0
    counts, rest = [largest] + [least] * (count - 1), total - largest - least * (count - 1)
    while rest > 0:
        candidates = [i for i in range(1, count) if counts[i] < largest] or [i for i in range(1, count) if counts[i] < reach]
        whole, budget = sum([loads[i] for i in candidates]), rest
        for i in candidates:
            extra = min(reach - counts[i], max(1, budget * loads[i] // whole), rest)
            counts[i] = counts[i] + extra
            rest = rest - extra
    return np.array(counts)


def bell_draw(stream_key, dims, spread, reach, shards=(), held_as=jnp.bfloat16):
    values = jax.random.normal(stream_key, dims, jnp.float32) * spread
    if len(shards) > 0:
        values = block_scale(stream_key, dims, shards, -0.22, 0.18) * values
    return jnp.clip(values, min=-reach, max=reach).astype(held_as)


def setup_inputs(seed: int = 0) -> dict:
    key_list = jax.random.split(jax.random.key(seed), 12)
    hidden = bell_draw(key_list[0], (SEQS, SEQ, D), 1.0, 6.0, ((0, 8), (1, 4)))
    queries = draw_queries(jax.random.fold_in(key_list[11], 71), 0)
    keys = draw_keys(jax.random.fold_in(key_list[11], 71), 0)
    values = bell_draw(key_list[3], (SEQS, SEQ, KVH * DH), 4.0, 24.0, ((0, 8), (1, 4)))
    out_weight = bell_draw(key_list[4], (HQ * DH, D), (HQ * DH) ** -0.5, 0.09375, ((1, 4),))
    norm_gain = jnp.clip(1.0 + 0.18 * jax.random.normal(key_list[5], (D,), jnp.float32), 0.1, 1.9)
    routes_keys = jax.random.split(jax.random.fold_in(key_list[6], 1), SEQS * SEQ // TOK_DEV)
    routes_turns = jax.random.permutation(jax.random.fold_in(key_list[6], 3), SEQS * SEQ // TOK_DEV)
    routes = jax.vmap(lambda own, number: routed_block(jax.random.fold_in(key_list[6], 2), own, number, TOK_DEV, EXPERTS, TOP, CAP, 2))(routes_keys, routes_turns).reshape((SEQS, SEQ, TOP))
    slot_scores = jnp.clip(jnp.exp(math.log(1.0) - 2.3025851 * jax.random.uniform(key_list[7], (SEQS, SEQ, TOP), jnp.float32) ** block_scale(key_list[7], (SEQS, SEQ, TOP), ((0, 8), (1, 4)), -0.2, 0.2)), 0.1, 1.0)
    gate_weight = bell_draw(key_list[8], (EXPERTS, D, HID), D ** -0.5, 0.09375, ((0, 32),))
    up_weight = bell_draw(key_list[9], (EXPERTS, D, HID), D ** -0.5, 0.09375, ((0, 32),))
    down_weight = bell_draw(key_list[10], (EXPERTS, HID, D), HID ** -0.5, 0.21875, ((0, 32),))
    return {"hidden": hidden, "queries": queries, "keys": keys, "values": values, "out_weight": out_weight, "norm_gain": norm_gain, "routes": routes, "slot_scores": slot_scores, "gate_weight": gate_weight, "up_weight": up_weight, "down_weight": down_weight}


def expert_ffn(inputs, w_gate, w_up, w_down):
    gated = jnp.dot(inputs, w_gate, preferred_element_type=jnp.float32)
    lifted = jnp.dot(inputs, w_up, preferred_element_type=jnp.float32)
    activated = (jax.nn.silu(gated) * lifted).astype(jnp.bfloat16)
    return jnp.dot(activated, w_down, preferred_element_type=jnp.float32).astype(jnp.bfloat16)

def attend(triple):
    query_rows, key_rows, value_rows = triple
    group_size = HQ // KVH
    length = query_rows.shape[0]
    query_four = query_rows.reshape(length, KVH, group_size, DH).astype(jnp.float32)
    key_three = key_rows.reshape(length, KVH, DH).astype(jnp.float32)
    value_three = value_rows.reshape(length, KVH, DH).astype(jnp.float32)
    scores = jnp.einsum('qkgd,jkd->kgqj', query_four, key_three) * DH ** (-0.5)
    position = jnp.arange(length)
    causal = position[None, :] <= position[:, None]
    scores = jnp.where(causal, scores, -1e+30)
    row_max = lax.optimization_barrier(jnp.max(scores, axis=-1, keepdims=True))
    weights = jnp.where(causal, jnp.exp(scores - row_max), 0.0)
    total_weight = lax.optimization_barrier(jnp.sum(weights, axis=-1))
    rounded = lax.optimization_barrier(weights.astype(jnp.bfloat16)).astype(jnp.float32)
    numerator = jnp.einsum('kgqj,jkd->kgqd', rounded, value_three)
    attended = numerator / total_weight[..., None]
    return jnp.transpose(attended, (2, 0, 1, 3)).reshape(length, HQ * DH).astype(jnp.bfloat16)

def block_ranks(block_ids):
    one_hot = (block_ids[:, None] == jnp.arange(EXPERTS)[None, :]).astype(jnp.int32)
    earlier = jnp.cumsum(one_hot, axis=0) - one_hot
    return lax.optimization_barrier(jnp.sum(earlier * one_hot, axis=1)).astype(jnp.int32)

def reference(hidden, queries, keys, values, out_weight, norm_gain, routes, slot_scores, gate_weight, up_weight, down_weight):
    tokens_all = SEQS * SEQ
    attended = lax.map(attend, (queries, keys, values))
    projected = jnp.dot(attended.reshape(tokens_all, HQ * DH), out_weight, preferred_element_type=jnp.float32).astype(jnp.bfloat16)
    residual = hidden.reshape(tokens_all, D).astype(jnp.float32) + projected.astype(jnp.float32)
    normed = (residual * lax.rsqrt(lax.optimization_barrier(jnp.mean(residual * residual, axis=1, keepdims=True)) + 1e-06) * norm_gain).astype(jnp.bfloat16)
    scores_flat = slot_scores.reshape(tokens_all, TOP)
    slot_gates = scores_flat / lax.optimization_barrier(jnp.sum(scores_flat, axis=1, keepdims=True))
    flat_gates = slot_gates.reshape(tokens_all * TOP)
    blocks = N_DP * N_CTX
    expert_of = routes.reshape(blocks, TOK_DEV * TOP).astype(jnp.int32)
    ranks = lax.map(block_ranks, expert_of)
    block_of = jnp.broadcast_to(jnp.arange(blocks, dtype=jnp.int32)[:, None], (blocks, TOK_DEV * TOP))
    row_in = block_of * CAP + ranks
    entry = jnp.arange(tokens_all * TOP, dtype=jnp.int32).reshape(blocks, TOK_DEV * TOP)
    table = jnp.full((EXPERTS, blocks * CAP), tokens_all * TOP, jnp.int32)
    table = table.at[expert_of.reshape(-1), row_in.reshape(-1)].set(entry.reshape(-1))

    def per_expert(combined, inputs):
        table_row, w_gate, w_up, w_down = inputs
        filled = table_row < tokens_all * TOP
        safe = jnp.where(filled, table_row, 0).astype(jnp.int32)
        token_index = (safe // TOP).astype(jnp.int32)
        expert_out = expert_ffn(normed[token_index], w_gate, w_up, w_down)
        weight = jnp.where(filled, flat_gates[safe], 0.0)
        combined = combined.at[token_index].add(weight[:, None] * expert_out.astype(jnp.float32))
        return (combined, None)
    combined, _ = lax.scan(per_expert, jnp.zeros((tokens_all, D), jnp.float32), (table, gate_weight, up_weight, down_weight))
    return (residual + combined).astype(jnp.bfloat16).reshape(SEQS, SEQ, D)
```

```python
import jax
import jax.numpy as jnp
from jax import lax
from jax.sharding import PartitionSpec as P

HQ = 32
KVH = 2
DH = 128
TOP = 8


def expert_ffn(slots_in, w_gate, w_up, w_down):
    flat_rows = slots_in.reshape(-1, slots_in.shape[-1])
    gated = jnp.dot(flat_rows, w_gate, preferred_element_type=jnp.float32)
    lifted = jnp.dot(flat_rows, w_up, preferred_element_type=jnp.float32)
    activated = (jax.nn.silu(gated) * lifted).astype(jnp.bfloat16)
    result = jnp.dot(activated, w_down, preferred_element_type=jnp.float32).astype(jnp.bfloat16)
    return result.reshape(slots_in.shape)


def local(
    hidden,
    queries,
    keys,
    values,
    out_weight,
    norm_gain,
    routes,
    slot_scores,
    gate_weight,
    up_weight,
    down_weight,
):
    tok_count = hidden.shape[1]
    model_width = hidden.shape[2]
    group_size = HQ // KVH
    score_scale = DH ** (-0.5)
    ctx_index = lax.axis_index("ctx")
    query_rows = queries[0].reshape(tok_count, KVH, group_size, DH)
    query_pos = ctx_index * tok_count + jnp.arange(tok_count, dtype=jnp.int32)
    key_piece = lax.all_gather(keys, "ctx", axis=1, tiled=True)
    value_piece = lax.all_gather(values, "ctx", axis=1, tiled=True)
    key_count = key_piece.shape[1]
    key_rows = key_piece[0].reshape(key_count, KVH, DH)
    value_rows = value_piece[0].reshape(key_count, KVH, DH)
    key_pos = jnp.arange(key_count, dtype=jnp.int32)
    running_max = jnp.full((KVH, group_size, tok_count), -1e30, jnp.float32)
    scores = (
        jnp.einsum("qkgd,jkd->kgqj", query_rows, key_rows, preferred_element_type=jnp.float32)
        * score_scale
    )
    causal = key_pos[None, :] <= query_pos[:, None]
    scores = jnp.where(causal, scores, -1e30)
    new_max = jnp.maximum(running_max, jnp.max(scores, axis=-1))
    weights = jnp.where(causal, jnp.exp(scores - new_max[..., None]), 0.0)
    running_sum = jnp.sum(weights, axis=-1)
    numerator = jnp.einsum(
        "kgqj,jkd->kgqd",
        weights.astype(jnp.bfloat16),
        value_rows,
        preferred_element_type=jnp.float32,
    )
    running_max, running_sum, numerator = (new_max, running_sum, numerator)
    attended = numerator / running_sum[..., None]
    attended = (
        jnp.transpose(attended, (2, 0, 1, 3)).reshape(tok_count, HQ * DH).astype(jnp.bfloat16)
    )
    columns = jnp.dot(
        lax.all_gather(attended, "ctx", axis=0, tiled=True),
        out_weight,
        preferred_element_type=jnp.float32,
    ).astype(jnp.bfloat16)
    projected = lax.all_to_all(columns, "ctx", split_axis=0, concat_axis=1, tiled=True)
    residual = hidden[0].astype(jnp.float32) + projected.astype(jnp.float32)
    normed = (
        residual
        * lax.rsqrt(jnp.mean(residual * residual, axis=1, keepdims=True) + 1e-06)
        * norm_gain
    ).astype(jnp.bfloat16)
    score_rows = slot_scores[0]
    slot_gates = score_rows / jnp.sum(score_rows, axis=1, keepdims=True)
    expert_total = lax.axis_size(("dp", "ctx"))
    capacity = max(2, tok_count * TOP * 9 // (8 * expert_total))
    named = routes[0][:, :, None] == jnp.arange(expert_total, dtype=jnp.int32)
    chosen = jnp.any(named, axis=1)
    gate_of = jnp.sum(jnp.where(named, slot_gates[:, :, None], 0.0), axis=1)
    row = jnp.arange(tok_count, dtype=jnp.int32)
    before = (row[None, :] < row[:, None]).astype(jnp.bfloat16)
    rank = jnp.dot(before, chosen.astype(jnp.bfloat16), preferred_element_type=jnp.float32)
    rank = jnp.where(chosen, rank.astype(jnp.int32), -1)
    place = rank.T[:, None, :] == jnp.arange(capacity, dtype=jnp.int32)[None, :, None]
    pick = place.astype(jnp.bfloat16).reshape(expert_total * capacity, tok_count)
    outgoing = jnp.dot(pick, normed, preferred_element_type=jnp.float32).astype(jnp.bfloat16)
    outgoing = outgoing.reshape(expert_total, capacity, model_width)
    served = expert_ffn(
        lax.all_to_all(outgoing, ("dp", "ctx"), split_axis=0, concat_axis=0, tiled=True),
        gate_weight[0],
        up_weight[0],
        down_weight[0],
    )
    returned = lax.all_to_all(served, ("dp", "ctx"), split_axis=0, concat_axis=0, tiled=True)
    returned = returned.reshape(expert_total * capacity, model_width)
    blend = jnp.where(place, gate_of.T[:, None, :], 0.0).reshape(expert_total * capacity, tok_count)
    high = blend.astype(jnp.bfloat16)
    low = (blend - high.astype(jnp.float32)).astype(jnp.bfloat16)
    over_slots = (((0,), (0,)), ((), ()))
    mixture = lax.dot_general(
        high, returned, over_slots, preferred_element_type=jnp.float32
    ) + lax.dot_general(low, returned, over_slots, preferred_element_type=jnp.float32)
    return (residual + mixture).astype(jnp.bfloat16)[None]


def solution(mesh):
    return jax.shard_map(
        local,
        mesh=mesh,
        in_specs=(
            P("dp", "ctx", None),
            P("dp", "ctx", None),
            P("dp", "ctx", None),
            P("dp", "ctx", None),
            P(None, "ctx"),
            P(),
            P("dp", "ctx", None),
            P("dp", "ctx", None),
            P(("dp", "ctx"), None, None),
            P(("dp", "ctx"), None, None),
            P(("dp", "ctx"), None, None),
        ),
        out_specs=P("dp", "ctx", None),
        check_vma=False,
    )
```

```python
import functools

import jax
import jax.numpy as jnp
from jax import lax
from jax.experimental import pallas as pl
from jax.experimental.pallas import tpu as pltpu
from jax.sharding import PartitionSpec as P

HQ = 32
KVH = 2
DH = 128
TOP = 8
MESH = pl.DeviceIdType.MESH


def _ceil(count, unit):
    return -(-count // unit) * unit


def _tiles(rows, cols, mt, nt, body):
    def step(i, carry):
        m, n = i // (cols // nt), i % (cols // nt)
        body(pl.ds(pl.multiple_of(m * mt, mt), mt), pl.ds(pl.multiple_of(n * nt, nt), nt))
        return carry

    lax.fori_loop(0, (rows // mt) * (cols // nt), step, 0)


def _moe_kernel(
    dims,
    normed,
    residual,
    pick,
    spread,
    gate_rows,
    w_gate,
    w_up,
    w_down,
    out,
    tokens,
    sent,
    got,
    gated,
    lifted,
    act,
    partials,
    wgu,
    wd,
    z_send,
    z_recv,
    x_send,
    x_recv,
    p_send,
    p_recv,
    w_sem,
    d_sem,
    credit,
):
    planes, ctx_n, chunks, tok, slots = dims
    peers = 2 * ctx_n
    rows = peers * slots
    dc = normed.shape[1] // chunks
    hid = gated.shape[1]
    mt = rows // 4
    nt = min(256, dc)
    dp, cx = lax.axis_index("dp"), lax.axis_index("ctx")
    z, core = dp // 2, dp % 2
    me = core * ctx_n + cx

    def in_plane(j):
        j = lax.rem(j + peers, peers)
        return (2 * z + j // ctx_n, lax.rem(j, ctx_n))

    def along(q):
        return (2 * lax.rem(q + planes, planes) + core, cx)

    def dot(a, b):
        return jnp.dot(a, b, preferred_element_type=jnp.float32)

    def load_gu(c):
        return [
            pltpu.make_async_copy(
                w.at[0, pl.ds(c * dc, dc), :], wgu.at[c % 2, i], w_sem.at[c % 2, i]
            )
            for i, w in enumerate((w_gate, w_up))
        ]

    def load_down(c):
        return pltpu.make_async_copy(
            w_down.at[0, :, pl.ds(c * dc, dc)], wd.at[c % 2], d_sem.at[c % 2]
        )

    def z_copy(c, q):
        return pltpu.make_async_remote_copy(
            src_ref=tokens.at[c, pl.ds(0, tok)],
            dst_ref=tokens.at[c, pl.ds(q * tok, tok)],
            send_sem=z_send.at[c, q - 1],
            recv_sem=z_recv.at[c, q - 1],
            device_id=along(z + q),
            device_id_type=MESH,
        )

    def x_copy(c, k, back):
        return pltpu.make_async_remote_copy(
            src_ref=sent.at[c, pl.ds(k * slots, slots)],
            dst_ref=got.at[c, pl.ds(k * slots, slots)],
            send_sem=x_send.at[c, k - 1],
            recv_sem=x_recv.at[c, k - 1],
            device_id=in_plane(me - k if back else me + k),
            device_id_type=MESH,
        )

    def p_copy(c, q):
        return pltpu.make_async_remote_copy(
            src_ref=tokens.at[c, pl.ds(q * tok, tok)],
            dst_ref=partials.at[c, pl.ds((q - 1) * tok, tok)],
            send_sem=p_send.at[c, q - 1],
            recv_sem=p_recv.at[c, q - 1],
            device_id=along(z - q),
            device_id_type=MESH,
        )

    for c in range(min(2, chunks)):
        for copy in load_gu(c):
            copy.start()
        load_down(c).start()
    for c in range(chunks):
        tokens[c, pl.ds(0, tok), :] = normed[:, pl.ds(c * dc, dc)]
    barrier = pltpu.get_barrier_semaphore()
    for q in range(1, planes):
        pl.semaphore_signal(barrier, inc=1, device_id=along(z + q), device_id_type=MESH)
    for k in range(1, peers):
        pl.semaphore_signal(barrier, inc=1, device_id=in_plane(me + k), device_id_type=MESH)
    pl.semaphore_wait(barrier, planes - 1 + peers - 1)
    for c in range(chunks):
        for q in range(1, planes):
            z_copy(c, q).start()

    def enter(c):
        for k in range(1, peers):
            x_copy(c, k, False).wait_recv()
        for copy in load_gu(c):
            copy.wait()

        def body(m, n):
            x = got[c, m, :]
            g = dot(x, wgu[c % 2, 0, :, n])
            u = dot(x, wgu[c % 2, 1, :, n])
            if c == 0:
                gated[m, n] = g
                lifted[m, n] = u
            elif c < chunks - 1:
                gated[m, n] += g
                lifted[m, n] += u
            else:
                g = g + gated[m, n]
                u = u + lifted[m, n]
                act[m, n] = (g / (1.0 + jnp.exp(-g)) * u).astype(jnp.bfloat16)

        _tiles(rows, hid, mt, min(256, hid), body)
        if c + 2 < chunks:
            for copy in load_gu(c + 2):
                copy.start()

    for c in range(chunks):
        for q in range(1, planes):
            z_copy(c, q).wait_recv()

        def body(m, n, c=c):
            sent[c, m, n] = dot(pick[m, :], tokens[c, :, n]).astype(jnp.bfloat16)

        _tiles(rows, dc, mt, nt, body)
        for k in range(1, peers):
            x_copy(c, k, False).start()
        got[c, pl.ds(0, slots), :] = sent[c, pl.ds(0, slots), :]
        if c > 0:
            enter(c - 1)
    enter(chunks - 1)
    for k in range(1, peers):
        pl.semaphore_signal(credit, inc=1, device_id=in_plane(me + k), device_id_type=MESH)

    def leave(c):
        for k in range(1, peers):
            x_copy(c, k, True).wait_recv()
        for q in range(1, planes):
            z_copy(c, q).wait_send()

        def body(m, n):
            tokens[c, m, n] = dot(spread[m, :], got[c, :, n]).astype(jnp.bfloat16)

        _tiles(planes * tok, dc, tok, nt, body)
        for q in range(1, planes):
            p_copy(c, q).start()

    for c in range(chunks):
        for k in range(1, peers):
            x_copy(c, k, False).wait_send()
        load_down(c).wait()

        def body(m, n, c=c):
            y = dot(act[m, :], wd[c % 2, :, n]) * gate_rows[m, :]
            sent[c, m, n] = y.astype(jnp.bfloat16)

        _tiles(rows, dc, mt, nt, body)
        if c + 2 < chunks:
            load_down(c + 2).start()
        if c == 0:
            pl.semaphore_wait(credit, peers - 1)
        for k in range(1, peers):
            x_copy(c, k, True).start()
        got[c, pl.ds(0, slots), :] = sent[c, pl.ds(0, slots), :]
        if c > 0:
            leave(c - 1)
    leave(chunks - 1)
    for c in range(chunks):
        for q in range(1, planes):
            p_copy(c, q).wait_recv()
        total = residual[:, pl.ds(c * dc, dc)] + tokens[c, pl.ds(0, tok), :].astype(jnp.float32)
        for q in range(1, planes):
            total += partials[c, pl.ds((q - 1) * tok, tok), :].astype(jnp.float32)
        out[:, pl.ds(c * dc, dc)] = total.astype(jnp.bfloat16)
    for c in range(chunks):
        for k in range(1, peers):
            x_copy(c, k, True).wait_send()
        for q in range(1, planes):
            p_copy(c, q).wait_send()


def moe(planes, ctx_n, slots, normed, residual, pick, spread, gate_rows, w_gate, w_up, w_down):
    tok, width = normed.shape
    hid = w_gate.shape[2]
    chunks = max(4, planes)
    peers = 2 * ctx_n
    rows = peers * slots
    dc = width // chunks
    dims = (planes, ctx_n, chunks, tok, slots)
    vmem = pl.BlockSpec(memory_space=pltpu.VMEM)
    hbm = pl.BlockSpec(memory_space=pl.ANY)
    dma = pltpu.SemaphoreType.DMA
    return pl.pallas_call(
        functools.partial(_moe_kernel, dims),
        out_shape=jax.ShapeDtypeStruct((tok, width), jnp.bfloat16),
        in_specs=[vmem] * 5 + [hbm] * 3,
        out_specs=vmem,
        scratch_shapes=[
            pltpu.VMEM((chunks, planes * tok, dc), jnp.bfloat16),
            pltpu.VMEM((chunks, rows, dc), jnp.bfloat16),
            pltpu.VMEM((chunks, rows, dc), jnp.bfloat16),
            pltpu.VMEM((rows, hid), jnp.float32),
            pltpu.VMEM((rows, hid), jnp.float32),
            pltpu.VMEM((rows, hid), jnp.bfloat16),
            pltpu.VMEM((chunks, (planes - 1) * tok, dc), jnp.bfloat16),
            pltpu.VMEM((2, 2, dc, hid), jnp.bfloat16),
            pltpu.VMEM((2, hid, dc), jnp.bfloat16),
            dma((chunks, planes - 1)),
            dma((chunks, planes - 1)),
            dma((chunks, peers - 1)),
            dma((chunks, peers - 1)),
            dma((chunks, planes - 1)),
            dma((chunks, planes - 1)),
            dma((2, 2)),
            dma((2,)),
            pltpu.SemaphoreType.REGULAR,
        ],
        compiler_params=pltpu.CompilerParams(
            collective_id=0, has_side_effects=True, vmem_limit_bytes=62 * 1024 * 1024
        ),
        cost_estimate=pl.CostEstimate(
            flops=6 * rows * width * hid, bytes_accessed=6 * width * hid, transcendentals=rows * hid
        ),
    )(normed, residual, pick, spread, gate_rows, w_gate, w_up, w_down)


def slot_places(named, before, capacity):
    rank = jnp.einsum(
        "kqs,st->kqt", named.astype(jnp.bfloat16), before, preferred_element_type=jnp.float32
    ).astype(jnp.int32)
    first = (jnp.arange(named.shape[1], dtype=jnp.int32) * capacity)[None, :, None]
    return jnp.where(named, rank + first, -1).reshape(named.shape[0], -1)


def countdown(blocks, start):
    count = blocks.shape[0]
    back = jnp.flip(blocks, 0)
    return lax.dynamic_slice_in_dim(jnp.concatenate([back, back]), count - 1 - start, count)


def tables(routes, slot_gates, capacity):
    tok = routes.shape[0]
    dp_n, ctx_n = lax.axis_size("dp"), lax.axis_size("ctx")
    planes, peers = dp_n // 2, 2 * ctx_n
    slots = _ceil(planes * capacity, 16)
    dp, cx = lax.axis_index("dp"), lax.axis_index("ctx")
    z, me = dp // 2, (dp % 2) * ctx_n + cx
    ids = lax.all_gather(routes.T, ("dp", "ctx"), axis=0).reshape(planes, peers, TOP, tok)
    gates = lax.all_gather(slot_gates.T, ("dp", "ctx"), axis=0).reshape(planes, peers, TOP, tok)
    k = jnp.arange(peers, dtype=jnp.int32)
    row = jnp.arange(tok, dtype=jnp.int32)
    before = (row[:, None] < row[None, :]).astype(jnp.bfloat16)
    slot = jnp.arange(slots, dtype=jnp.int32)[None, :, None]
    ids, gates = countdown(ids, z), countdown(gates, z)
    mine = lax.dynamic_index_in_dim(ids, me, 1, keepdims=False)
    target = z * peers + (me + k) % peers
    named = jnp.any(mine[None] == target[:, None, None, None], axis=2)
    pick = slot_places(named, before, capacity)[:, None, :] == slot
    pick = pick.astype(jnp.bfloat16).reshape(peers * slots, planes * tok)
    hit = ids == z * peers + me
    named = countdown(jnp.any(hit, axis=2).transpose(1, 0, 2), me)
    gate = countdown(jnp.sum(jnp.where(hit, gates, 0.0), axis=2).transpose(1, 0, 2), me)
    arrives = slot_places(named, before, capacity)[:, None, :] == slot
    gate = gate.reshape(peers, 1, planes * tok)
    gate_rows = jnp.sum(jnp.where(arrives, gate, 0.0), axis=2).reshape(peers * slots, 1)
    return planes, ctx_n, slots, pick, pick.T, gate_rows


def local(
    hidden,
    queries,
    keys,
    values,
    out_weight,
    norm_gain,
    routes,
    slot_scores,
    gate_weight,
    up_weight,
    down_weight,
):
    tok_count = hidden.shape[1]
    model_width = hidden.shape[2]
    group_size = HQ // KVH
    score_scale = DH ** (-0.5)
    ctx_index = lax.axis_index("ctx")
    query_rows = queries[0].reshape(tok_count, KVH, group_size, DH)
    query_pos = ctx_index * tok_count + jnp.arange(tok_count, dtype=jnp.int32)
    key_piece = lax.all_gather(keys, "ctx", axis=1, tiled=True)
    value_piece = lax.all_gather(values, "ctx", axis=1, tiled=True)
    key_count = key_piece.shape[1]
    key_rows = key_piece[0].reshape(key_count, KVH, DH)
    value_rows = value_piece[0].reshape(key_count, KVH, DH)
    key_pos = jnp.arange(key_count, dtype=jnp.int32)
    running_max = jnp.full((KVH, group_size, tok_count), -1e30, jnp.float32)
    scores = (
        jnp.einsum("qkgd,jkd->kgqj", query_rows, key_rows, preferred_element_type=jnp.float32)
        * score_scale
    )
    causal = key_pos[None, :] <= query_pos[:, None]
    scores = jnp.where(causal, scores, -1e30)
    new_max = jnp.maximum(running_max, jnp.max(scores, axis=-1))
    weights = jnp.where(causal, jnp.exp(scores - new_max[..., None]), 0.0)
    running_sum = jnp.sum(weights, axis=-1)
    numerator = jnp.einsum(
        "kgqj,jkd->kgqd",
        weights.astype(jnp.bfloat16),
        value_rows,
        preferred_element_type=jnp.float32,
    )
    running_max, running_sum, numerator = (new_max, running_sum, numerator)
    attended = numerator / running_sum[..., None]
    attended = (
        jnp.transpose(attended, (2, 0, 1, 3)).reshape(tok_count, HQ * DH).astype(jnp.bfloat16)
    )
    columns = jnp.dot(
        lax.all_gather(attended, "ctx", axis=0, tiled=True),
        out_weight,
        preferred_element_type=jnp.float32,
    ).astype(jnp.bfloat16)
    projected = lax.all_to_all(columns, "ctx", split_axis=0, concat_axis=1, tiled=True)
    residual = hidden[0].astype(jnp.float32) + projected.astype(jnp.float32)
    normed = (
        residual
        * lax.rsqrt(jnp.mean(residual * residual, axis=1, keepdims=True) + 1e-06)
        * norm_gain
    ).astype(jnp.bfloat16)
    score_rows = slot_scores[0]
    slot_gates = score_rows / jnp.sum(score_rows, axis=1, keepdims=True)
    expert_total = lax.axis_size(("dp", "ctx"))
    capacity = max(2, tok_count * TOP * 9 // (8 * expert_total))
    planes, ctx_n, slots, pick, spread, gate_rows = tables(routes[0], slot_gates, capacity)
    return moe(
        planes,
        ctx_n,
        slots,
        normed,
        residual,
        pick,
        spread,
        gate_rows,
        gate_weight,
        up_weight,
        down_weight,
    )[None]


def solution(mesh):
    return jax.shard_map(
        local,
        mesh=mesh,
        in_specs=(
            P("dp", "ctx", None),
            P("dp", "ctx", None),
            P("dp", "ctx", None),
            P("dp", "ctx", None),
            P(None, "ctx"),
            P(),
            P("dp", "ctx", None),
            P("dp", "ctx", None),
            P(("dp", "ctx"), None, None),
            P(("dp", "ctx"), None, None),
            P(("dp", "ctx"), None, None),
        ),
        out_specs=P("dp", "ctx", None),
        check_vma=False,
    )
```

```python
import functools

import jax
import jax.numpy as jnp
from jax import lax
from jax.experimental import pallas as pl
from jax.experimental.pallas import tpu as pltpu
from jax.sharding import PartitionSpec as P

HQ = 32
KVH = 2
DH = 128
TOP = 8
AHEAD = 2
MESH = pl.DeviceIdType.MESH


def _ceil(count, unit):
    return -(-count // unit) * unit


def _tiles(rows, cols, mt, nt, body):
    def step(i, carry):
        m, n = i // (cols // nt), i % (cols // nt)
        body(pl.ds(pl.multiple_of(m * mt, mt), mt), pl.ds(pl.multiple_of(n * nt, nt), nt))
        return carry

    lax.fori_loop(0, (rows // mt) * (cols // nt), step, 0)


def _moe_kernel(
    dims,
    normed,
    residual,
    pick,
    spread,
    w_gate,
    w_up,
    w_down,
    out,
    tokens,
    sent,
    got,
    gated,
    lifted,
    act,
    partials,
    wgu,
    wd,
    z_send,
    z_recv,
    x_send,
    x_recv,
    p_send,
    p_recv,
    w_sem,
    d_sem,
    credit,
):
    planes, ctx_n, chunks, tok, slots = dims
    peers = 2 * ctx_n
    rows = peers * slots
    dc = normed.shape[1] // chunks
    hid = gated.shape[1]
    mt = rows // 4
    nt = min(256, dc)
    dp, cx = lax.axis_index("dp"), lax.axis_index("ctx")
    z, core = dp // 2, dp % 2
    me = core * ctx_n + cx

    def in_plane(j):
        j = lax.rem(j + peers, peers)
        return (2 * z + j // ctx_n, lax.rem(j, ctx_n))

    def along(q):
        return (2 * lax.rem(q + planes, planes) + core, cx)

    def dot(a, b):
        return jnp.dot(a, b, preferred_element_type=jnp.float32)

    def load_gu(c):
        return [
            pltpu.make_async_copy(
                w.at[0, pl.ds(c * dc, dc), :], wgu.at[c % 2, i], w_sem.at[c % 2, i]
            )
            for i, w in enumerate((w_gate, w_up))
        ]

    def load_down(c):
        return pltpu.make_async_copy(
            w_down.at[0, :, pl.ds(c * dc, dc)], wd.at[c % 2], d_sem.at[c % 2]
        )

    def z_copy(c, q):
        return pltpu.make_async_remote_copy(
            src_ref=tokens.at[c, pl.ds(0, tok)],
            dst_ref=tokens.at[c, pl.ds(q * tok, tok)],
            send_sem=z_send.at[c, q - 1],
            recv_sem=z_recv.at[c, q - 1],
            device_id=along(z + q),
            device_id_type=MESH,
        )

    def x_copy(c, k, back):
        return pltpu.make_async_remote_copy(
            src_ref=sent.at[c, pl.ds(k * slots, slots)],
            dst_ref=got.at[c, pl.ds(k * slots, slots)],
            send_sem=x_send.at[c, k - 1],
            recv_sem=x_recv.at[c, k - 1],
            device_id=in_plane(me - k if back else me + k),
            device_id_type=MESH,
        )

    def p_copy(c, q):
        return pltpu.make_async_remote_copy(
            src_ref=tokens.at[c, pl.ds(q * tok, tok)],
            dst_ref=partials.at[c, pl.ds((q - 1) * tok, tok)],
            send_sem=p_send.at[c, q - 1],
            recv_sem=p_recv.at[c, q - 1],
            device_id=along(z - q),
            device_id_type=MESH,
        )

    for c in range(min(2, chunks)):
        for copy in load_gu(c):
            copy.start()
        load_down(c).start()
    for c in range(chunks):
        tokens[c, pl.ds(0, tok), :] = normed[:, pl.ds(c * dc, dc)]
    barrier = pltpu.get_barrier_semaphore()
    for q in range(1, planes):
        pl.semaphore_signal(barrier, inc=1, device_id=along(z + q), device_id_type=MESH)
    for k in range(1, peers):
        pl.semaphore_signal(barrier, inc=1, device_id=in_plane(me + k), device_id_type=MESH)
    pl.semaphore_wait(barrier, planes - 1 + peers - 1)
    for c in range(min(AHEAD, chunks)):
        for q in range(1, planes):
            z_copy(c, q).start()

    def enter(c):
        for k in range(1, peers):
            x_copy(c, k, False).wait_recv()
        for copy in load_gu(c):
            copy.wait()

        def body(m, n):
            x = got[c, m, :]
            g = dot(x, wgu[c % 2, 0, :, n])
            u = dot(x, wgu[c % 2, 1, :, n])
            if c == 0:
                gated[m, n] = g
                lifted[m, n] = u
            elif c < chunks - 1:
                gated[m, n] += g
                lifted[m, n] += u
            else:
                g = g + gated[m, n]
                u = u + lifted[m, n]
                act[m, n] = (g / (1.0 + jnp.exp(-g)) * u).astype(jnp.bfloat16)

        _tiles(rows, hid, mt, min(256, hid), body)
        if c + 2 < chunks:
            for copy in load_gu(c + 2):
                copy.start()

    for c in range(chunks):
        for q in range(1, planes):
            z_copy(c, q).wait_recv()
        if c + AHEAD < chunks:
            for q in range(1, planes):
                z_copy(c + AHEAD, q).start()

        def body(m, n, c=c):
            sent[c, m, n] = dot(pick[m, :], tokens[c, :, n]).astype(jnp.bfloat16)

        _tiles(rows, dc, mt, nt, body)
        for k in range(1, peers):
            x_copy(c, k, False).start()
        got[c, pl.ds(0, slots), :] = sent[c, pl.ds(0, slots), :]
        if c > 0:
            enter(c - 1)
    enter(chunks - 1)
    for k in range(1, peers):
        pl.semaphore_signal(credit, inc=1, device_id=in_plane(me + k), device_id_type=MESH)

    def leave(c):
        for k in range(1, peers):
            x_copy(c, k, True).wait_recv()
        for q in range(1, planes):
            z_copy(c, q).wait_send()

        def body(m, n):
            tokens[c, m, n] = dot(spread[m, :], got[c, :, n]).astype(jnp.bfloat16)

        _tiles(planes * tok, dc, tok, nt, body)
        for q in range(1, planes):
            p_copy(c, q).start()

    for c in range(chunks):
        for k in range(1, peers):
            x_copy(c, k, False).wait_send()
        load_down(c).wait()

        def body(m, n, c=c):
            sent[c, m, n] = dot(act[m, :], wd[c % 2, :, n]).astype(jnp.bfloat16)

        _tiles(rows, dc, mt, nt, body)
        if c + 2 < chunks:
            load_down(c + 2).start()
        if c == 0:
            pl.semaphore_wait(credit, peers - 1)
        for k in range(1, peers):
            x_copy(c, k, True).start()
        got[c, pl.ds(0, slots), :] = sent[c, pl.ds(0, slots), :]
        if c > 0:
            leave(c - 1)
    leave(chunks - 1)
    for c in range(chunks):
        for q in range(1, planes):
            p_copy(c, q).wait_recv()
        total = residual[:, pl.ds(c * dc, dc)] + tokens[c, pl.ds(0, tok), :].astype(jnp.float32)
        for q in range(1, planes):
            total += partials[c, pl.ds((q - 1) * tok, tok), :].astype(jnp.float32)
        out[:, pl.ds(c * dc, dc)] = total.astype(jnp.bfloat16)
    for c in range(chunks):
        for k in range(1, peers):
            x_copy(c, k, True).wait_send()
        for q in range(1, planes):
            p_copy(c, q).wait_send()


def moe(planes, ctx_n, slots, normed, residual, pick, spread, w_gate, w_up, w_down):
    tok, width = normed.shape
    hid = w_gate.shape[2]
    chunks = max(8, planes)
    peers = 2 * ctx_n
    rows = peers * slots
    dc = width // chunks
    dims = (planes, ctx_n, chunks, tok, slots)
    vmem = pl.BlockSpec(memory_space=pltpu.VMEM)
    hbm = pl.BlockSpec(memory_space=pl.ANY)
    dma = pltpu.SemaphoreType.DMA
    return pl.pallas_call(
        functools.partial(_moe_kernel, dims),
        out_shape=jax.ShapeDtypeStruct((tok, width), jnp.bfloat16),
        in_specs=[vmem] * 4 + [hbm] * 3,
        out_specs=vmem,
        scratch_shapes=[
            pltpu.VMEM((chunks, planes * tok, dc), jnp.bfloat16),
            pltpu.VMEM((chunks, rows, dc), jnp.bfloat16),
            pltpu.VMEM((chunks, rows, dc), jnp.bfloat16),
            pltpu.VMEM((rows, hid), jnp.float32),
            pltpu.VMEM((rows, hid), jnp.float32),
            pltpu.VMEM((rows, hid), jnp.bfloat16),
            pltpu.VMEM((chunks, (planes - 1) * tok, dc), jnp.bfloat16),
            pltpu.VMEM((2, 2, dc, hid), jnp.bfloat16),
            pltpu.VMEM((2, hid, dc), jnp.bfloat16),
            dma((chunks, planes - 1)),
            dma((chunks, planes - 1)),
            dma((chunks, peers - 1)),
            dma((chunks, peers - 1)),
            dma((chunks, planes - 1)),
            dma((chunks, planes - 1)),
            dma((2, 2)),
            dma((2,)),
            pltpu.SemaphoreType.REGULAR,
        ],
        compiler_params=pltpu.CompilerParams(
            collective_id=0, has_side_effects=True, vmem_limit_bytes=62 * 1024 * 1024
        ),
        cost_estimate=pl.CostEstimate(
            flops=6 * rows * width * hid, bytes_accessed=6 * width * hid, transcendentals=rows * hid
        ),
    )(normed, residual, pick, spread, w_gate, w_up, w_down)


def slot_places(named, before, capacity):
    rank = jnp.einsum(
        "kqs,st->kqt", named.astype(jnp.bfloat16), before, preferred_element_type=jnp.float32
    ).astype(jnp.int32)
    first = (jnp.arange(named.shape[1], dtype=jnp.int32) * capacity)[None, :, None]
    return jnp.where(named, rank + first, -1).reshape(named.shape[0], -1)


def countdown(blocks, start):
    count = blocks.shape[0]
    back = jnp.flip(blocks, 0)
    return lax.dynamic_slice_in_dim(jnp.concatenate([back, back]), count - 1 - start, count)


def tables(routes, slot_gates, capacity):
    tok = routes.shape[0]
    dp_n, ctx_n = lax.axis_size("dp"), lax.axis_size("ctx")
    planes, peers = dp_n // 2, 2 * ctx_n
    slots = _ceil(planes * capacity, 16)
    dp, cx = lax.axis_index("dp"), lax.axis_index("ctx")
    z, me = dp // 2, (dp % 2) * ctx_n + cx
    both = jnp.concatenate([routes.T.astype(jnp.float32), slot_gates.T])
    column = [[2 * p + core for p in range(planes)] for core in range(2)]
    both = lax.all_gather(both, "dp", axis=0, axis_index_groups=column)
    both = countdown(both, z)
    ids, gates = both[:, :TOP].astype(jnp.int32), both[:, TOP:]
    k = jnp.arange(peers, dtype=jnp.int32)
    row = jnp.arange(tok, dtype=jnp.int32)
    before = (row[:, None] < row[None, :]).astype(jnp.bfloat16)
    slot = jnp.arange(slots, dtype=jnp.int32)[None, :, None]
    target = z * peers + (me + k) % peers
    hit = ids[None] == target[:, None, None, None]
    named = jnp.any(hit, axis=2)
    gate = jnp.sum(jnp.where(hit, gates[None], 0.0), axis=2).reshape(peers, 1, planes * tok)
    pick = slot_places(named, before, capacity)[:, None, :] == slot
    spread = jnp.where(pick, gate, 0.0).astype(jnp.bfloat16)
    pick = pick.astype(jnp.bfloat16).reshape(peers * slots, planes * tok)
    return planes, ctx_n, slots, pick, spread.reshape(peers * slots, planes * tok).T


def local(
    hidden,
    queries,
    keys,
    values,
    out_weight,
    norm_gain,
    routes,
    slot_scores,
    gate_weight,
    up_weight,
    down_weight,
):
    tok_count = hidden.shape[1]
    model_width = hidden.shape[2]
    group_size = HQ // KVH
    score_scale = DH ** (-0.5)
    ctx_index = lax.axis_index("ctx")
    query_rows = queries[0].reshape(tok_count, KVH, group_size, DH)
    query_pos = ctx_index * tok_count + jnp.arange(tok_count, dtype=jnp.int32)
    pair = lax.all_gather(jnp.concatenate([keys, values], 2), "ctx", axis=1, tiled=True)
    key_piece, value_piece = jnp.split(pair, 2, axis=2)
    key_count = key_piece.shape[1]
    key_rows = key_piece[0].reshape(key_count, KVH, DH)
    value_rows = value_piece[0].reshape(key_count, KVH, DH)
    key_pos = jnp.arange(key_count, dtype=jnp.int32)
    running_max = jnp.full((KVH, group_size, tok_count), -1e30, jnp.float32)
    scores = (
        jnp.einsum("qkgd,jkd->kgqj", query_rows, key_rows, preferred_element_type=jnp.float32)
        * score_scale
    )
    causal = key_pos[None, :] <= query_pos[:, None]
    scores = jnp.where(causal, scores, -1e30)
    new_max = jnp.maximum(running_max, jnp.max(scores, axis=-1))
    weights = jnp.where(causal, jnp.exp(scores - new_max[..., None]), 0.0)
    running_sum = jnp.sum(weights, axis=-1)
    numerator = jnp.einsum(
        "kgqj,jkd->kgqd",
        weights.astype(jnp.bfloat16),
        value_rows,
        preferred_element_type=jnp.float32,
    )
    running_max, running_sum, numerator = (new_max, running_sum, numerator)
    attended = numerator / running_sum[..., None]
    attended = (
        jnp.transpose(attended, (2, 0, 1, 3)).reshape(tok_count, HQ * DH).astype(jnp.bfloat16)
    )
    columns = jnp.dot(
        lax.all_gather(attended, "ctx", axis=0, tiled=True),
        out_weight,
        preferred_element_type=jnp.float32,
    ).astype(jnp.bfloat16)
    projected = lax.all_to_all(columns, "ctx", split_axis=0, concat_axis=1, tiled=True)
    residual = hidden[0].astype(jnp.float32) + projected.astype(jnp.float32)
    normed = (
        residual
        * lax.rsqrt(jnp.mean(residual * residual, axis=1, keepdims=True) + 1e-06)
        * norm_gain
    ).astype(jnp.bfloat16)
    score_rows = slot_scores[0]
    slot_gates = score_rows / jnp.sum(score_rows, axis=1, keepdims=True)
    expert_total = lax.axis_size(("dp", "ctx"))
    capacity = max(2, tok_count * TOP * 9 // (8 * expert_total))
    planes, ctx_n, slots, pick, spread = tables(routes[0], slot_gates, capacity)
    return moe(
        planes,
        ctx_n,
        slots,
        normed,
        residual,
        pick,
        spread,
        gate_weight,
        up_weight,
        down_weight,
    )[None]


def solution(mesh):
    return jax.shard_map(
        local,
        mesh=mesh,
        in_specs=(
            P("dp", "ctx", None),
            P("dp", "ctx", None),
            P("dp", "ctx", None),
            P("dp", "ctx", None),
            P(None, "ctx"),
            P(),
            P("dp", "ctx", None),
            P("dp", "ctx", None),
            P(("dp", "ctx"), None, None),
            P(("dp", "ctx"), None, None),
            P(("dp", "ctx"), None, None),
        ),
        out_specs=P("dp", "ctx", None),
        check_vma=False,
    )
```
